32 devices in a mesh: attn: 4 (over z), expert: 8 (over y, x, core).
Axes of the slice: x: 2, y: 2, z: 4, core: 2. Of those that a mesh axis runs over, the one named last changes fastest.
Arguments:
- stream_in: bfloat16 [256, 4096], P(('attn', 'expert')), may hold values from -48 to 48
- norm_gain: bfloat16 [4096], replicated, may hold values from 0.5 to 1.5
- expert_ids: int32 [256, 8], P(('attn', 'expert')), may hold values from 0 to 31, as said below
- route_weights: float32 [256, 8], P(('attn', 'expert')), may hold values from 0.1 to 1
- w_gate: bfloat16 [32, 1536, 4096], P('expert', 'attn'), may hold values from -0.09375 to 0.09375
- w_up: bfloat16 [32, 1536, 4096], P('expert', 'attn'), may hold values from -0.09375 to 0.09375
- w_down: bfloat16 [32, 1536, 4096], P('expert', 'attn'), may hold values from -0.15625 to 0.15625
Outputs:
- expert_mix: float32 [256, 4096], P(('attn', 'expert'))
The draws below stay inside these ranges and needn't reach their ends.
Inputs may be any that keep to these rules, and one draw needn't show every extreme that they name: `expert_ids`: each row names 8 different experts; the tokens of one device name no expert more than 4 times, and one expert is named exactly 4 times by the tokens of every device.
All inputs are finite; a program needn't handle non-finite values.
Results may differ from the reference program's by a relative error of at most 0.014.
Values may be sent and summed in bfloat16 or wider, within the bound.
No kernel may reach another device: no remote copies, remote signals or barrier semaphores. Data moves between devices by JAX's collectives and lax.ppermute only.
A program may use at most 128 MiB of HBM per device.

```python
import math
import jax
import jax.numpy as jnp
from jax import lax

D = 4096
FF = 1536
TOP = 8
ROWS = 8
EXPERTS = 32
TOKENS = 256
MOST = 4
SLICE = 384
N_ATTN = 4
N_EXPERT = 8


def log_uniform(key, shape, lower, upper):
    return jnp.exp(jax.random.uniform(key, shape, jnp.float32, jnp.log(lower), jnp.log(upper)))


def draw_stream_in(key, part):
    keys = jax.random.split(key, 3)
    column_scale = log_uniform(keys[1], (1, D), 0.3, 3.0)
    base = jnp.clip(jax.random.normal(keys[0], (TOKENS, D), jnp.float32), -4.0, 4.0)
    row_scale = log_uniform(keys[2], (TOKENS, 1), 0.3, 3.0)
    return (base * row_scale * column_scale).astype(jnp.bfloat16)


def random_order(key, blocks, count):
    scores = jax.random.randint(key, (blocks, count), 0, 1 << 20) * count + jnp.arange(count, dtype=jnp.int32)[None, :]
    return jnp.argsort(scores, axis=1).astype(jnp.int32)


def draw_expert_ids(key, part):
    blocks = TOKENS // ROWS
    others_count = EXPERTS - 3
    keys = jax.random.split(key, 8)
    first = jax.random.randint(keys[0], (EXPERTS,), 0, 1 << 20) * EXPERTS + jnp.arange(EXPERTS, dtype=jnp.int32)
    order = jnp.argsort(first).astype(jnp.int32)
    hottest = order[:3]
    others = order[3:]
    listed = others[random_order(keys[1], blocks, others_count)]
    repeats = TOP * ROWS // others_count + 2
    tiled = jnp.tile(listed, (1, repeats))
    rank_one = jnp.argsort(random_order(keys[2], blocks, ROWS), axis=1).astype(jnp.int32)
    rank_two = jnp.argsort(random_order(keys[3], blocks, ROWS), axis=1).astype(jnp.int32)
    rank_three = jnp.argsort(random_order(keys[4], blocks, ROWS), axis=1).astype(jnp.int32)
    count_two = jax.random.randint(keys[5], (blocks, 1), 0, MOST + 1)
    count_three = jax.random.randint(keys[6], (blocks, 1), 0, MOST + 1)
    flags = jnp.stack([(rank_one < MOST).astype(jnp.int32), (rank_two < count_two).astype(jnp.int32), (rank_three < count_three).astype(jnp.int32)], axis=2)
    hot_count = jnp.sum(flags, axis=2)
    length = TOP - hot_count
    begin = jnp.cumsum(length, axis=1) - length
    place = jnp.cumsum(flags, axis=2) - flags
    column = jnp.arange(TOP, dtype=jnp.int32)
    where_listed = jnp.clip(begin[:, :, None] + column[None, None, :] - hot_count[:, :, None], 0, None)
    from_list = jnp.take_along_axis(tiled, where_listed.reshape(blocks, ROWS * TOP), axis=1).reshape(blocks, ROWS, TOP)
    hot_entry = jnp.zeros((blocks, ROWS, TOP), jnp.int32)
    for which in range(3):
        taken = (flags[:, :, which:which + 1] == 1) & (place[:, :, which:which + 1] == column[None, None, :])
        hot_entry = hot_entry + jnp.where(taken, hottest[which], 0)
    chosen = jnp.where(column[None, None, :] < hot_count[:, :, None], hot_entry, from_list)
    rotate = jax.random.randint(keys[7], (blocks, ROWS, 1), 0, TOP)
    chosen = jnp.take_along_axis(chosen, (column[None, None, :] + rotate) % TOP, axis=2)
    return chosen.reshape(TOKENS, TOP).astype(jnp.int32)


def level_of(own_key, shape, pieces, smallest, high):
    gain = 1.0
    for position, shards_of in pieces:
        heights = jax.random.uniform(jax.random.fold_in(jax.random.fold_in(own_key, 6), position), (shards_of,), jnp.float32, smallest / len(pieces), high / len(pieces))
        gain = gain * jnp.repeat(jnp.exp(heights), shape[position] // shards_of).reshape((-1,) + (1,) * (len(shape) - 1 - position))
    return gain


def bell_draw(key, extent, deviation, bound, cuts=(), held_as=jnp.bfloat16):
    result = deviation * jax.random.normal(key, extent, jnp.float32)
    if cuts:
        result = result * level_of(key, extent, cuts, -0.22, 0.18)
    return jnp.clip(result, -bound, bound).astype(held_as)


def setup_inputs(seed: int = 0) -> dict:
    splits = jax.random.split(jax.random.key(seed), 8)
    stream_in = draw_stream_in(jax.random.fold_in(splits[7], 71), 0)
    norm_gain = jnp.clip(jax.random.uniform(splits[1], (D,), jnp.float32, 0.5, 1.5), 0.5, 1.5).astype(jnp.bfloat16)
    expert_ids = draw_expert_ids(jax.random.fold_in(splits[7], 71), 0)
    route_weights = jnp.clip(jnp.exp(math.log(1.0) - 2.3025851 * jax.random.uniform(splits[3], (TOKENS, TOP), jnp.float32) ** level_of(splits[3], (TOKENS, TOP), ((0, 32),), -0.2, 0.2)), 0.1, 1.0)
    w_gate = bell_draw(splits[4], (EXPERTS, FF, D), D ** -0.5, 0.09375, ((0, 8), (1, 4)))
    w_up = bell_draw(splits[5], (EXPERTS, FF, D), D ** -0.5, 0.09375, ((0, 8), (1, 4)))
    w_down = bell_draw(splits[6], (EXPERTS, FF, D), FF ** -0.5, 0.15625, ((0, 8), (1, 4)))
    return dict(stream_in=stream_in, norm_gain=norm_gain, expert_ids=expert_ids, route_weights=route_weights, w_gate=w_gate, w_up=w_up, w_down=w_down)


def reference(stream_in, norm_gain, expert_ids, route_weights, w_gate, w_up, w_down):
    device_count = N_ATTN * N_EXPERT
    stream = stream_in.astype(jnp.float32)
    inverse = lax.rsqrt(lax.optimization_barrier(jnp.mean(stream * stream, axis=-1, keepdims=True)) + 1e-06)
    normed = (stream * inverse * norm_gain.astype(jnp.float32)).astype(jnp.bfloat16)
    blocked_ids = expert_ids.reshape(device_count, ROWS, TOP)
    blocked_weights = route_weights.reshape(device_count, ROWS, TOP)
    blocked_rows = normed.reshape(device_count, ROWS, D).astype(jnp.float32)
    slot_range = jnp.arange(MOST, dtype=jnp.int32)

    def one_expert(totals, inputs):
        gate_matrix, up_matrix, down_matrix, index = inputs
        hit = blocked_ids == index
        named = jnp.any(hit, axis=-1).astype(jnp.int32)
        earlier = jnp.cumsum(named, axis=1) - named
        weight = lax.optimization_barrier(jnp.sum(jnp.where(hit, blocked_weights, jnp.zeros_like(blocked_weights)), axis=-1))
        select = ((named[:, :, None] == 1) & (earlier[:, :, None] == slot_range[None, None, :])).astype(jnp.float32)
        gathered = jnp.einsum('nrm,nrd->nmd', select, blocked_rows, precision=lax.Precision.HIGHEST)
        gathered = gathered.astype(jnp.bfloat16).reshape(device_count * MOST, D)
        gate = jnp.dot(gathered, gate_matrix.T, preferred_element_type=jnp.float32)
        up = jnp.dot(gathered, up_matrix.T, preferred_element_type=jnp.float32)
        act = (jax.nn.silu(gate) * up).astype(jnp.bfloat16)
        parts = jnp.einsum('rsf,sfd->rsd', act.reshape(device_count * MOST, N_ATTN, SLICE).astype(jnp.float32), down_matrix.reshape(N_ATTN, SLICE, D).astype(jnp.float32))
        rounded = lax.optimization_barrier(parts.astype(jnp.bfloat16)).astype(jnp.float32)
        outputs = lax.optimization_barrier(jnp.sum(rounded, axis=1)).reshape(device_count, MOST, D)
        mixer = select * weight[:, :, None]
        added = jnp.einsum('nrm,nmd->nrd', mixer, outputs, precision=lax.Precision.HIGHEST)
        return (totals + added, None)
    initial = jnp.zeros((device_count, ROWS, D), jnp.float32)
    totals, _ = lax.scan(one_expert, initial, (w_gate, w_up, w_down, jnp.arange(EXPERTS, dtype=jnp.int32)))
    return totals.reshape(TOKENS, D)
```

```python
import jax
import jax.numpy as jnp
from jax import lax
from jax.experimental import pallas as pl
from jax.experimental.pallas import tpu as pltpu
from jax.sharding import PartitionSpec as P

LANES = 128
F32 = jnp.float32
BF16 = jnp.bfloat16
MIB = 1 << 20


def whole(shape):
    return pl.BlockSpec(shape, lambda *_: (0,) * len(shape))


def swap(value, axis, distance):
    size = lax.axis_size(axis)
    return lax.ppermute(value, axis, [(i, i ^ distance) for i in range(size)])


def pack_kernel(stream_ref, gain_ref, ids_ref, weights_ref, out_ref, *, experts, features):
    stream = stream_ref[...].astype(F32)
    inverse = lax.rsqrt(jnp.mean(stream * stream, axis=-1, keepdims=True) + 1e-06)
    normed = stream * inverse * gain_ref[...].astype(F32)
    out_ref[:, :features] = normed.astype(BF16)
    rows = stream.shape[0]
    width = out_ref.shape[1] - features
    column = lax.broadcasted_iota(jnp.int32, (rows, width), 1)
    dense = jnp.zeros((rows, width), F32)
    for k in range(ids_ref.shape[1]):
        expert = ids_ref[:, k : k + 1]
        weight = weights_ref[:, k : k + 1]
        high = weight.astype(BF16).astype(F32)
        middle = (weight - high).astype(BF16).astype(F32)
        low = weight - high - middle
        dense = dense + jnp.where(column == expert, high, 0.0)
        dense = dense + jnp.where(column == expert + experts, middle, 0.0)
        dense = dense + jnp.where(column == expert + 2 * experts, low, 0.0)
    out_ref[:, features:] = dense.astype(BF16)


def hidden_kernel(*refs, pieces, features):
    piece_refs = refs[:pieces]
    gate_ref, up_ref, spread_ref, act_ref, rows_ref = refs[pieces:]
    step = pl.program_id(0)
    count = piece_refs[0].shape[0]

    @pl.when(step == 0)
    def _():
        for i, ref in enumerate(piece_refs):
            rows_ref[i * count : (i + 1) * count, :] = ref[...]

    rows = rows_ref[:, :features]
    matrix = jnp.concatenate([gate_ref[...], up_ref[...]], axis=0)
    both = lax.dot_general(rows, matrix, (((1,), (1,)), ((), ())), preferred_element_type=F32)
    weight = jnp.dot(rows_ref[:, features:], spread_ref[...], preferred_element_type=F32)
    block = gate_ref.shape[0]
    gate, up = both[:, :block], both[:, block:]
    act_ref[...] = (gate / (1.0 + jnp.exp(-gate)) * up * weight).astype(BF16)


def down_kernel(act_ref, down_ref, keep_ref, send_ref):
    out = jnp.dot(act_ref[...], down_ref[...], preferred_element_type=F32)
    half = keep_ref.shape[0]
    keep_ref[...] = out[:half]
    send_ref[...] = out[half:].astype(BF16)


def local(stream_in, norm_gain, expert_ids, route_weights, w_gate, w_up, w_down):
    row_count, features = stream_in.shape
    held, slice_size, _ = w_gate.shape
    attn_size = lax.axis_size("attn")
    expert_size = lax.axis_size("expert")
    experts = held * expert_size
    planes = expert_size // 2
    width = -(-3 * experts // LANES) * LANES
    hidden = held * slice_size

    packed = pl.pallas_call(
        lambda *refs: pack_kernel(*refs, experts=experts, features=features),
        out_shape=jax.ShapeDtypeStruct((row_count, features + width), BF16),
    )(stream_in, norm_gain.reshape(1, features), expert_ids, route_weights)

    column = jnp.concatenate([packed] + [swap(packed, "attn", d) for d in range(1, attn_size)], axis=0)
    pieces = [column] + [swap(column, "expert", 2 * d) for d in range(1, planes)]
    pieces = pieces + [swap(piece, "expert", 1) for piece in pieces]
    tokens = len(pieces) * column.shape[0]

    first = lax.axis_index("expert") * held
    lane = jnp.arange(width, dtype=jnp.int32)[:, None]
    owner = first + jnp.arange(hidden, dtype=jnp.int32)[None, :] // slice_size
    spread = ((lane % experts == owner) & (lane < 3 * experts)).astype(BF16)

    block = LANES
    act = pl.pallas_call(
        lambda *refs: hidden_kernel(*refs, pieces=len(pieces), features=features),
        out_shape=jax.ShapeDtypeStruct((tokens, hidden), BF16),
        grid=(hidden // block,),
        in_specs=[whole(column.shape)] * len(pieces)
        + [
            pl.BlockSpec((block, features), lambda j: (j, 0)),
            pl.BlockSpec((block, features), lambda j: (j, 0)),
            pl.BlockSpec((width, block), lambda j: (0, j)),
        ],
        out_specs=pl.BlockSpec((tokens, block), lambda j: (0, j)),
        scratch_shapes=[pltpu.VMEM((tokens, features + width), BF16)],
        compiler_params=pltpu.CompilerParams(vmem_limit_bytes=56 * MIB),
    )(*pieces, w_gate.reshape(hidden, features), w_up.reshape(hidden, features), spread)

    chunk = 512
    keep, send = pl.pallas_call(
        down_kernel,
        out_shape=(
            jax.ShapeDtypeStruct((tokens // 2, features), F32),
            jax.ShapeDtypeStruct((tokens // 2, features), BF16),
        ),
        grid=(features // chunk,),
        in_specs=[
            whole((tokens, hidden)),
            pl.BlockSpec((hidden, chunk), lambda j: (0, j)),
        ],
        out_specs=[
            pl.BlockSpec((tokens // 2, chunk), lambda j: (0, j)),
            pl.BlockSpec((tokens // 2, chunk), lambda j: (0, j)),
        ],
        compiler_params=pltpu.CompilerParams(vmem_limit_bytes=56 * MIB),
    )(act, w_down.reshape(hidden, features))

    total = keep + swap(send, "expert", 1).astype(F32)
    total = total.reshape(planes, attn_size * row_count, features)
    parts = [swap(total[d].astype(BF16), "expert", 2 * d) for d in range(1, planes)]
    total = sum([part.astype(F32) for part in parts], total[0])
    total = total.reshape(attn_size, row_count, features)
    parts = [swap(total[d].astype(BF16), "attn", d) for d in range(1, attn_size)]
    return sum([part.astype(F32) for part in parts], total[0])


def solution(mesh):
    return jax.shard_map(
        local,
        mesh=mesh,
        in_specs=(
            P(("attn", "expert"), None),
            P(),
            P(("attn", "expert"), None),
            P(("attn", "expert"), None),
            P("expert", "attn", None),
            P("expert", "attn", None),
            P("expert", "attn", None),
        ),
        out_specs=P(("attn", "expert"), None),
        check_vma=False,
    )
```

```python
import jax
import jax.numpy as jnp
from jax import lax
from jax.experimental import pallas as pl
from jax.experimental.pallas import tpu as pltpu
from jax.sharding import PartitionSpec as P

LANES = 128
F32 = jnp.float32
BF16 = jnp.bfloat16
MIB = 1 << 20
HALVES = 2
IN_VMEM = pl.BlockSpec(memory_space=pltpu.VMEM)
IN_HBM = pl.BlockSpec(memory_space=pltpu.HBM)
ANYWHERE = pl.BlockSpec(memory_space=pl.ANY)


def near(value):
    return pltpu.with_memory_space_constraint(value, pltpu.VMEM)


def far(value):
    return pltpu.with_memory_space_constraint(value, pltpu.HBM)


def swap(value, axis, to):
    return lax.ppermute(value, axis, [(i, to(i)) for i in range(lax.axis_size(axis))])


def partner(step, steps):
    return lambda i: i ^ (2 << (step if i % 2 == 0 else steps - 1 - step))


def pack_kernel(stream_ref, gain_ref, ids_ref, weights_ref, own_ref, *half_refs, experts):
    stream = stream_ref[...].astype(F32)
    inverse = lax.rsqrt(jnp.mean(stream * stream, axis=-1, keepdims=True) + 1e-06)
    rows, features = stream.shape
    for i in range(features // LANES):
        here = slice(i * LANES, (i + 1) * LANES)
        own_ref[:, here] = (stream[:, here] * inverse * gain_ref[i : i + 1, :].astype(F32)).astype(BF16)
    width = own_ref.shape[1] - features
    column = lax.broadcasted_iota(jnp.int32, (rows, width), 1)
    dense = jnp.zeros((rows, width), F32)
    for k in range(ids_ref.shape[1]):
        expert = ids_ref[:, k : k + 1]
        weight = weights_ref[:, k : k + 1]
        high = weight.astype(BF16).astype(F32)
        middle = (weight - high).astype(BF16).astype(F32)
        low = weight - high - middle
        dense = dense + jnp.where(column == expert, high, 0.0)
        dense = dense + jnp.where(column == expert + experts, middle, 0.0)
        dense = dense + jnp.where(column == expert + 2 * experts, low, 0.0)
    own_ref[:, features:] = dense.astype(BF16)
    at = 0
    for ref in half_refs:
        ref[...] = jnp.zeros_like(ref)
        ref[:rows, :] = own_ref[:, at : at + ref.shape[1]]
        at += ref.shape[1]


def load_kernel(*refs, sources, cuts):
    source_refs, out_refs, sems = refs[:sources], refs[-1 - len(cuts) : -1], refs[-1]
    copies = []
    for i, (source, at, size) in enumerate(cuts):
        copies.append(pltpu.make_async_copy(source_refs[source].at[:, pl.ds(at, size)], out_refs[i], sems.at[i]))
    for copy in copies:
        copy.start()
    for copy in copies:
        copy.wait()


def load(arrays, cuts, after):
    size = sum(arrays[s].shape[0] * n * 2 for s, _, n in cuts)
    out = pl.pallas_call(
        lambda *refs: load_kernel(*refs, sources=len(arrays), cuts=cuts),
        out_shape=[pltpu.VMEM((arrays[s].shape[0], n), BF16) for s, _, n in cuts],
        in_specs=[IN_HBM] * len(arrays) + [ANYWHERE],
        out_specs=[IN_VMEM] * len(cuts),
        scratch_shapes=[pltpu.SemaphoreType.DMA((len(cuts),))],
        compiler_params=pltpu.CompilerParams(vmem_limit_bytes=MIB),
        cost_estimate=pl.CostEstimate(flops=0, bytes_accessed=size, transcendentals=0),
    )(*[far(a) for a in arrays], after)
    return [near(value) for value in out]


def dot_rows(rows, matrix):
    return lax.dot_general(rows, matrix, (((1,), (1,)), ((), ())), preferred_element_type=F32)


def first_kernel(*refs, pieces, block, part, experts):
    piece_refs = refs[:pieces]
    gate_ref, up_ref, down_hbm, gate_out, up_out, spread_ref, down_ref, rows_ref, sem = refs[pieces:]
    fetch = pltpu.make_async_copy(down_hbm.at[:, pl.ds(0, part)], down_ref, sem)
    fetch.start()
    count = piece_refs[0].shape[0]
    for i, ref in enumerate(piece_refs):
        rows_ref[i * count : (i + 1) * count, :] = ref[...]
    for j in range(gate_ref.shape[0] // block):
        here = slice(j * block, (j + 1) * block)
        both = dot_rows(rows_ref[...], jnp.concatenate([gate_ref[here], up_ref[here]], axis=0))
        gate_out[:, here] = both[:, :block]
        up_out[:, here] = both[:, block:]
    held = experts // lax.axis_size("expert")
    lane = lax.broadcasted_iota(jnp.int32, spread_ref.shape, 0)
    unit = lax.broadcasted_iota(jnp.int32, spread_ref.shape, 1)
    low = (lax.axis_index("expert") * held + jnp.zeros((1, 1), jnp.int32)) + unit // (spread_ref.shape[1] // held)
    hit = (lane == low) | (lane == low + experts) | (lane == low + 2 * experts)
    spread_ref[...] = jnp.where(hit, 1.0, 0.0).astype(BF16)
    fetch.wait()


def second_kernel(*refs, pieces, block, part):
    piece_refs = refs[:pieces]
    gate_ref, up_ref, gate_in, up_in, spread_ref, down_hbm, act_ref, down_ref, rows_ref, sem = refs[pieces:]
    fetch = pltpu.make_async_copy(down_hbm.at[:, pl.ds(part, part)], down_ref, sem)
    fetch.start()
    count = piece_refs[0].shape[0]
    for i, ref in enumerate(piece_refs):
        rows_ref[i * count : (i + 1) * count, :] = ref[...]
    for j in range(gate_ref.shape[0] // block):
        here = slice(j * block, (j + 1) * block)
        both = dot_rows(rows_ref[:, :part], jnp.concatenate([gate_ref[here], up_ref[here]], axis=0))
        weight = jnp.dot(rows_ref[:, part:], spread_ref[:, here], preferred_element_type=F32)
        gate = gate_in[:, here] + both[:, :block]
        up = up_in[:, here] + both[:, block:]
        act_ref[:, here] = (gate / (1.0 + jnp.exp(-gate)) * up * weight).astype(BF16)
    fetch.wait()


def down_kernel(act_ref, down_ref, keep_ref, send_ref, *, chunk):
    half = keep_ref.shape[0]
    for j in range(keep_ref.shape[1] // chunk):
        here = slice(j * chunk, (j + 1) * chunk)
        out = jnp.dot(act_ref[...], down_ref[:, here], preferred_element_type=F32)
        keep_ref[:, here] = out[:half]
        send_ref[:, here] = out[half:].astype(BF16)


def params(mib):
    return pltpu.CompilerParams(vmem_limit_bytes=mib * MIB)


def cost(flops, size):
    return pl.CostEstimate(flops=flops, bytes_accessed=size, transcendentals=0)


def local(stream_in, norm_gain, expert_ids, route_weights, w_gate, w_up, w_down):
    row_count, features = stream_in.shape
    held, slice_size, _ = w_gate.shape
    attn_size = lax.axis_size("attn")
    expert_size = lax.axis_size("expert")
    experts = held * expert_size
    width = -(-3 * experts // LANES) * LANES
    hidden = held * slice_size
    part = features // HALVES
    tokens = row_count * attn_size * expert_size
    half = tokens // 2
    steps = (expert_size // 2).bit_length() - 1
    beside = lambda i: i ^ 1

    w_gate = w_gate.reshape(hidden, features)
    w_up = w_up.reshape(hidden, features)
    w_down = w_down.reshape(hidden, features)

    own, *columns = pl.pallas_call(
        lambda *refs: pack_kernel(*refs, experts=experts),
        out_shape=[
            pltpu.VMEM((row_count, features + width), BF16),
            pltpu.VMEM((row_count * attn_size, part), BF16),
            pltpu.VMEM((row_count * attn_size, part + width), BF16),
        ],
    )(stream_in, norm_gain.reshape(features // LANES, LANES), expert_ids, route_weights)

    received = [swap(own, "attn", lambda i, d=d: (i + d) % attn_size) for d in range(1, attn_size)]
    gate_1, up_1 = load([w_gate, w_up], [(0, 0, part), (1, 0, part)], own)
    *received, gate_1, up_1 = lax.optimization_barrier((*received, gate_1, up_1))
    for d, value in enumerate(received, 1):
        at = d * row_count
        columns[0] = columns[0].at[at : at + row_count].set(value[:, :part])
        columns[1] = columns[1].at[at : at + row_count].set(value[:, part:])

    (gate_2,) = load([w_gate], [(0, part, part)], columns[1])
    def beside_all(pieces):
        return pieces + [swap(piece, "expert", beside) for piece in pieces]

    first_column, second_column = columns
    for step in range(steps - 1):
        other = swap(first_column, "expert", partner(step, steps))
        if step == 0:
            other, gate_2 = lax.optimization_barrier((other, gate_2))
        first_column = jnp.concatenate([first_column, other], axis=0)
        other = swap(second_column, "expert", partner(step, steps))
        second_column = jnp.concatenate([second_column, other], axis=0)
    (up_2,) = load([w_up], [(0, part, part)], first_column)
    other = swap(first_column, "expert", partner(steps - 1, steps))
    other, up_2 = lax.optimization_barrier((other, up_2))
    first_pieces = beside_all([first_column, other])
    other = swap(second_column, "expert", partner(steps - 1, steps))
    pieces = len(first_pieces)

    gate, up, spread, down_1 = pl.pallas_call(
        lambda *refs: first_kernel(*refs, pieces=pieces, block=LANES, part=part, experts=experts),
        out_shape=[pltpu.VMEM((tokens, hidden), F32)] * 2
        + [pltpu.VMEM((width, hidden), BF16), pltpu.VMEM((hidden, part), BF16)],
        in_specs=[IN_VMEM] * (pieces + 2) + [IN_HBM],
        out_specs=[IN_VMEM] * 4,
        scratch_shapes=[pltpu.VMEM((tokens, part), BF16), pltpu.SemaphoreType.DMA],
        compiler_params=params(6),
        cost_estimate=cost(4 * tokens * hidden * part, 4 * hidden * part),
    )(*first_pieces, near(gate_1), near(up_1), far(w_down))
    other, gate, up = lax.optimization_barrier((other, gate, up))
    second_pieces = beside_all([second_column, other])
    act, down_2 = pl.pallas_call(
        lambda *refs: second_kernel(*refs, pieces=pieces, block=LANES, part=part),
        out_shape=[pltpu.VMEM((tokens, hidden), BF16), pltpu.VMEM((hidden, part), BF16)],
        in_specs=[IN_VMEM] * (pieces + 5) + [IN_HBM],
        out_specs=[IN_VMEM] * 2,
        scratch_shapes=[pltpu.VMEM((tokens, part + width), BF16), pltpu.SemaphoreType.DMA],
        compiler_params=params(6),
        cost_estimate=cost(4 * tokens * hidden * part, 4 * hidden * part),
    )(*second_pieces, near(gate_2), near(up_2), near(gate), near(up), near(spread), far(w_down))

    outs = []
    for down in (down_1, down_2):
        keep, send = pl.pallas_call(
            lambda *refs: down_kernel(*refs, chunk=512),
            out_shape=[
                pltpu.VMEM((half, part), F32),
                pltpu.VMEM((half, part), BF16),
            ],
            in_specs=[IN_VMEM] * 2,
            out_specs=[IN_VMEM] * 2,
            compiler_params=params(12),
            cost_estimate=cost(2 * tokens * hidden * part, 2 * hidden * part),
        )(near(act), near(down))
        total = keep + swap(send, "expert", beside).astype(F32)
        for step in reversed(range(steps)):
            count = total.shape[0] // 2
            back = swap(total[count:].astype(BF16), "expert", partner(step, steps))
            total = total[:count] + back.astype(F32)
        outs.append(total)
    total = jnp.concatenate(outs, axis=1).reshape(attn_size, row_count, features)
    back = [
        swap(total[d].astype(BF16), "attn", lambda i, d=d: (i - d) % attn_size) for d in range(1, attn_size)
    ]
    return sum([value.astype(F32) for value in back], total[0])


def solution(mesh):
    return jax.shard_map(
        local,
        mesh=mesh,
        in_specs=(
            P(("attn", "expert"), None),
            P(),
            P(("attn", "expert"), None),
            P(("attn", "expert"), None),
            P("expert", "attn", None),
            P("expert", "attn", None),
            P("expert", "attn", None),
        ),
        out_specs=P(("attn", "expert"), None),
        check_vma=False,
    )
```

```python
import jax
import jax.numpy as jnp
from jax import lax
from jax.experimental import pallas as pl
from jax.experimental.pallas import tpu as pltpu
from jax.sharding import PartitionSpec as P

LANES = 128
F32 = jnp.float32
BF16 = jnp.bfloat16
MIB = 1 << 20
HALVES = 2
DOWNS = 1
COSTS = False
LOADS = True
CUT = 2048
Z_UP = False
P1_WHOLE = False
Z_HALVES = False
IN_VMEM = pl.BlockSpec(memory_space=pltpu.VMEM)
IN_HBM = pl.BlockSpec(memory_space=pltpu.HBM)
ANYWHERE = pl.BlockSpec(memory_space=pl.ANY)


def near(value):
    return pltpu.with_memory_space_constraint(value, pltpu.VMEM)


def far(value):
    return pltpu.with_memory_space_constraint(value, pltpu.HBM)


def swap(value, axis, to):
    return lax.ppermute(value, axis, [(i, to(i)) for i in range(lax.axis_size(axis))])


def partner(step, steps):
    return lambda i: i ^ (2 << (step if i % 2 == 0 else steps - 1 - step))


def fold(total, step, steps):
    count = total.shape[0] // 2
    back = swap(total[count:].astype(BF16), "expert", partner(step, steps))
    return total[:count] + back.astype(F32)


def pack_kernel(stream_ref, gain_ref, ids_ref, weights_ref, own_ref, *half_refs, experts):
    stream = stream_ref[...].astype(F32)
    inverse = lax.rsqrt(jnp.mean(stream * stream, axis=-1, keepdims=True) + 1e-06)
    rows, features = stream.shape
    for i in range(features // LANES):
        here = slice(i * LANES, (i + 1) * LANES)
        own_ref[:, here] = (stream[:, here] * inverse * gain_ref[i : i + 1, :].astype(F32)).astype(BF16)
    width = own_ref.shape[1] - features
    column = lax.broadcasted_iota(jnp.int32, (rows, width), 1)
    dense = jnp.zeros((rows, width), F32)
    for k in range(ids_ref.shape[1]):
        expert = ids_ref[:, k : k + 1]
        weight = weights_ref[:, k : k + 1]
        high = weight.astype(BF16).astype(F32)
        middle = (weight - high).astype(BF16).astype(F32)
        low = weight - high - middle
        dense = dense + jnp.where(column == expert, high, 0.0)
        dense = dense + jnp.where(column == expert + experts, middle, 0.0)
        dense = dense + jnp.where(column == expert + 2 * experts, low, 0.0)
    own_ref[:, features:] = dense.astype(BF16)
    at = 0
    for ref in half_refs:
        ref[...] = jnp.zeros_like(ref)
        ref[:rows, :] = own_ref[:, at : at + ref.shape[1]]
        at += ref.shape[1]


def load_kernel(*refs, sources, cuts, experts):
    source_refs, sems = refs[:sources], refs[-1]
    out_refs = refs[sources + 1 : -1]
    copies = []
    for i, (source, at, size) in enumerate(cuts):
        copies.append(pltpu.make_async_copy(source_refs[source].at[:, pl.ds(at, size)], out_refs[i], sems.at[i]))
    for copy in copies:
        copy.start()
    if experts:
        spread_ref = out_refs[-1]
        held = experts // lax.axis_size("expert")
        lane = lax.broadcasted_iota(jnp.int32, spread_ref.shape, 0)
        unit = lax.broadcasted_iota(jnp.int32, spread_ref.shape, 1)
        owner = lax.axis_index("expert") * held + unit // (spread_ref.shape[1] // held)
        hit = (lane == owner) | (lane == owner + experts) | (lane == owner + 2 * experts)
        spread_ref[...] = jnp.where(hit, 1.0, 0.0).astype(BF16)
    for copy in copies:
        copy.wait()


def load(arrays, cuts, after, experts=0, width=0):
    rows = arrays[0].shape[0]
    size = sum(rows * n * 2 for _, _, n in cuts)
    return pl.pallas_call(
        lambda *refs: load_kernel(*refs, sources=len(arrays), cuts=cuts, experts=experts),
        out_shape=[pltpu.VMEM((rows, n), BF16) for _, _, n in cuts] + [pltpu.VMEM((width, rows), BF16)] * bool(experts),
        in_specs=[IN_HBM] * len(arrays) + [ANYWHERE],
        out_specs=[IN_VMEM] * (len(cuts) + bool(experts)),
        scratch_shapes=[pltpu.SemaphoreType.DMA((len(cuts),))],
        compiler_params=pltpu.CompilerParams(vmem_limit_bytes=MIB),
        cost_estimate=pl.CostEstimate(flops=0, bytes_accessed=size if LOADS else 0, transcendentals=0),
    )(*[far(a) for a in arrays], after)


def dot_rows(rows, matrix):
    return lax.dot_general(rows, matrix, (((1,), (1,)), ((), ())), preferred_element_type=F32)


def gate_up(rows, gate_ref, up_ref, at, block):
    here = slice(at, at + block)
    both = dot_rows(rows, jnp.concatenate([gate_ref[here], up_ref[here]], axis=0))
    return both[:, :block], both[:, block:]


def first_kernel(*refs, pieces, block):
    piece_refs = refs[:pieces]
    gate_ref, up_ref, rows_ref, gate_out, up_out = refs[pieces:]
    count = piece_refs[0].shape[0]
    for i, ref in enumerate(piece_refs):
        rows_ref[i * count : (i + 1) * count, :] = ref[...]
    for j in range(0, gate_out.shape[1], block):
        gate_out[:, j : j + block], up_out[:, j : j + block] = gate_up(rows_ref[...], gate_ref, up_ref, j, block)


def middle_kernel(rows_ref, gate_ref, up_ref, gate_out, up_out, *, block, start):
    for j in range(0, gate_out.shape[1], block):
        gate_out[:, j : j + block], up_out[:, j : j + block] = gate_up(
            rows_ref[...], gate_ref, up_ref, start + j, block
        )


def second_kernel(*refs, pieces, block, part, start, size):
    piece_refs = refs[:pieces]
    gate_ref, up_ref, *sums, spread_ref, down_hbm, act_ref, down_ref, rows_ref, sem = refs[pieces:]
    fetch = pltpu.make_async_copy(down_hbm.at[:, pl.ds(start, size)], down_ref, sem)
    fetch.start()
    count = piece_refs[0].shape[0]
    for i, ref in enumerate(piece_refs):
        rows_ref[i * count : (i + 1) * count, :] = ref[...]
    cut = sums[0].shape[1]
    for j in range(0, gate_ref.shape[0], block):
        here = slice(j, j + block)
        gate, up = gate_up(rows_ref[:, :part], gate_ref, up_ref, j, block)
        weight = jnp.dot(rows_ref[:, part:], spread_ref[:, here], preferred_element_type=F32)
        gate_in, up_in = sums[:2] if j < cut else sums[2:]
        there = slice(j % cut, j % cut + block)
        gate, up = gate + gate_in[:, there], up + up_in[:, there]
        act_ref[:, here] = (gate / (1.0 + jnp.exp(-gate)) * up * weight).astype(BF16)
    fetch.wait()


def down_kernel(act_ref, down_ref, keep_ref, send_ref, *, chunk, start):
    half = keep_ref.shape[0]
    for j in range(keep_ref.shape[1] // chunk):
        here = slice(j * chunk, (j + 1) * chunk)
        there = slice(start + j * chunk, start + (j + 1) * chunk)
        out = jnp.dot(act_ref[...], down_ref[:, there], preferred_element_type=F32)
        keep_ref[:, here] = out[:half]
        send_ref[:, here] = out[half:].astype(BF16)


def params(mib):
    return pltpu.CompilerParams(vmem_limit_bytes=mib * MIB)


def cost(flops, size):
    if not COSTS:
        flops, size = 0, 0
    return pl.CostEstimate(flops=flops, bytes_accessed=size, transcendentals=0)


def local(stream_in, norm_gain, expert_ids, route_weights, w_gate, w_up, w_down):
    row_count, features = stream_in.shape
    held, slice_size, _ = w_gate.shape
    attn_size = lax.axis_size("attn")
    expert_size = lax.axis_size("expert")
    experts = held * expert_size
    width = -(-3 * experts // LANES) * LANES
    hidden = held * slice_size
    part = features // HALVES
    tokens = row_count * attn_size * expert_size
    half = tokens // 2
    steps = (expert_size // 2).bit_length() - 1
    beside = lambda i: i ^ 1

    w_gate = w_gate.reshape(hidden, features)
    w_up = w_up.reshape(hidden, features)
    w_down = w_down.reshape(hidden, features)

    own, column = pl.pallas_call(
        lambda *refs: pack_kernel(*refs, experts=experts),
        out_shape=[
            pltpu.VMEM((row_count, features + width), BF16),
            pltpu.VMEM((row_count * attn_size, features + width), BF16),
        ],
    )(stream_in, norm_gain.reshape(features // LANES, LANES), expert_ids, route_weights)

    order = range(1, attn_size) if Z_UP else range(attn_size - 1, 0, -1)
    received = {d: swap(own, "attn", lambda i, d=d: (i + d) % attn_size) for d in order}
    gate_1, up_1 = load([w_gate, w_up], [(0, 0, part), (1, 0, part)], own)
    *values, gate_1, up_1 = lax.optimization_barrier((*received.values(), gate_1, up_1))
    for d, value in zip(received, values):
        column = column.at[d * row_count : (d + 1) * row_count].set(value)

    gate_2, up_2 = load([w_gate, w_up], [(0, part, part), (1, part, part)], column)
    for step in range(steps - 1):
        other = swap(column, "expert", partner(step, steps))
        if step == 0:
            other, gate_2, up_2 = lax.optimization_barrier((other, gate_2, up_2))
        column = jnp.concatenate([column, other], axis=0)
    columns = [column[:, :part], column[:, part:]]
    down_1, spread = load([w_down], [(0, 0, CUT)], columns[0], experts, width)
    others = [swap(value, "expert", partner(steps - 1, steps)) for value in columns]
    others[0], down_1, spread = lax.optimization_barrier((others[0], down_1, spread))

    def both_of_pair(pieces):
        return pieces + [swap(piece, "expert", beside) for piece in pieces]

    pieces = both_of_pair([columns[0], others[0]])
    count = len(pieces)
    cut = hidden // 2
    matmul = cost(2 * tokens * hidden * part, 2 * hidden * part)
    rows, gate_a, up_a = pl.pallas_call(
        lambda *refs: first_kernel(*refs, pieces=count, block=LANES),
        out_shape=[pltpu.VMEM((tokens, part), BF16)] + [pltpu.VMEM((tokens, cut), F32)] * 2,
        in_specs=[IN_VMEM] * (count + 2),
        out_specs=[IN_VMEM] * 3,
        compiler_params=params(6),
        cost_estimate=matmul,
    )(*pieces, near(gate_1), near(up_1))
    others[1], rows = lax.optimization_barrier((others[1], rows))
    gate_b, up_b = pl.pallas_call(
        lambda *refs: middle_kernel(*refs, block=LANES, start=cut),
        out_shape=[pltpu.VMEM((tokens, cut), F32)] * 2,
        in_specs=[IN_VMEM] * 3,
        out_specs=[IN_VMEM] * 2,
        compiler_params=params(6),
        cost_estimate=matmul,
    )(near(rows), near(gate_1), near(up_1))
    pieces = both_of_pair([columns[1], others[1]])
    act, down_2 = pl.pallas_call(
        lambda *refs: second_kernel(*refs, pieces=count, block=LANES, part=part, start=CUT, size=features - CUT),
        out_shape=[pltpu.VMEM((tokens, hidden), BF16), pltpu.VMEM((hidden, features - CUT), BF16)],
        in_specs=[IN_VMEM] * (count + 7) + [IN_HBM],
        out_specs=[IN_VMEM] * 2,
        scratch_shapes=[pltpu.VMEM((tokens, part + width), BF16), pltpu.SemaphoreType.DMA],
        compiler_params=params(6),
        cost_estimate=cost(4 * tokens * hidden * part, 4 * hidden * part),
    )(
        *pieces,
        near(gate_2),
        near(up_2),
        *[near(value) for value in (gate_a, up_a, gate_b, up_b)],
        near(spread),
        far(w_down),
    )

    outs = []
    for down in (down_1, down_2):
        size = down.shape[1] // DOWNS
        keeps, sends = [], []
        for i in range(DOWNS):
            keep, send = pl.pallas_call(
                lambda *refs, i=i: down_kernel(*refs, chunk=512, start=i * size),
                out_shape=[pltpu.VMEM((half, size), F32), pltpu.VMEM((half, size), BF16)],
                in_specs=[IN_VMEM] * 2,
                out_specs=[IN_VMEM] * 2,
                compiler_params=params(12),
                cost_estimate=cost(2 * tokens * hidden * size, 2 * hidden * size),
            )(near(act), near(down))
            keeps.append(keep)
            sends.append(swap(send, "expert", beside))
        keep, send = jnp.concatenate(keeps, axis=1), jnp.concatenate(sends, axis=1)
        total = keep + send.astype(F32)
        for step in reversed(range(1 if P1_WHOLE else 0, steps)):
            total = fold(total, step, steps)
        outs.append(total)
    if P1_WHOLE:
        outs = [fold(jnp.concatenate(outs, axis=1), 0, steps)]
    if not Z_HALVES:
        outs = [jnp.concatenate(outs, axis=1)]
    result = []
    for total in outs:
        total = total.reshape(attn_size, row_count, -1)
        back = [swap(total[d].astype(BF16), "attn", lambda i, d=d: (i - d) % attn_size) for d in order]
        result.append(sum([value.astype(F32) for value in back], total[0]))
    return jnp.concatenate(result, axis=1)


def solution(mesh):
    return jax.shard_map(
        local,
        mesh=mesh,
        in_specs=(
            P(("attn", "expert"), None),
            P(),
            P(("attn", "expert"), None),
            P(("attn", "expert"), None),
            P("expert", "attn", None),
            P("expert", "attn", None),
            P("expert", "attn", None),
        ),
        out_specs=P(("attn", "expert"), None),
        check_vma=False,
    )
```

```python
import jax
import jax.numpy as jnp
from jax import lax
from jax.experimental import pallas as pl
from jax.experimental.pallas import tpu as pltpu
from jax.sharding import PartitionSpec as P

LANES = 128
F32 = jnp.float32
BF16 = jnp.bfloat16
MIB = 1 << 20
AG_CUT = 1792
RS_CUTS = (2048, 2048)
ROWS_FIRST = 768
P1_SPLIT = False
AG_ORDER = (3, 2, 1)
RS_ORDER = (2, 1, 3)
XOR = False
IN_VMEM = pl.BlockSpec(memory_space=pltpu.VMEM)
IN_HBM = pl.BlockSpec(memory_space=pltpu.HBM)
ANYWHERE = pl.BlockSpec(memory_space=pl.ANY)


def near(value):
    return pltpu.with_memory_space_constraint(value, pltpu.VMEM)


def far(value):
    return pltpu.with_memory_space_constraint(value, pltpu.HBM)


def swap(value, axis, to):
    return lax.ppermute(value, axis, [(i, to(i)) for i in range(lax.axis_size(axis))])


def hop(distance, size):
    if XOR:
        return lambda i: i ^ abs(distance)
    return lambda i: (i + distance) % size


def order_of(order, size):
    return order if len(order) == size - 1 else range(size - 1, 0, -1)


def partner(step, steps):
    return lambda i: i ^ (2 << (step if i % 2 == 0 else steps - 1 - step))


def fold(total, step, steps):
    count = total.shape[0] // 2
    back = swap(total[count:].astype(BF16), "expert", partner(step, steps))
    return total[:count] + back.astype(F32)


def pack_kernel(stream_ref, gain_ref, ids_ref, weights_ref, own_ref, *half_refs, experts):
    stream = stream_ref[...].astype(F32)
    inverse = lax.rsqrt(jnp.mean(stream * stream, axis=-1, keepdims=True) + 1e-06)
    rows, features = stream.shape
    for i in range(features // LANES):
        here = slice(i * LANES, (i + 1) * LANES)
        own_ref[:, here] = (stream[:, here] * inverse * gain_ref[i : i + 1, :].astype(F32)).astype(BF16)
    width = own_ref.shape[1] - features
    column = lax.broadcasted_iota(jnp.int32, (rows, width), 1)
    dense = jnp.zeros((rows, width), F32)
    for k in range(ids_ref.shape[1]):
        expert = ids_ref[:, k : k + 1]
        weight = weights_ref[:, k : k + 1]
        high = weight.astype(BF16).astype(F32)
        middle = (weight - high).astype(BF16).astype(F32)
        low = weight - high - middle
        dense = dense + jnp.where(column == expert, high, 0.0)
        dense = dense + jnp.where(column == expert + experts, middle, 0.0)
        dense = dense + jnp.where(column == expert + 2 * experts, low, 0.0)
    own_ref[:, features:] = dense.astype(BF16)
    at = 0
    for ref in half_refs:
        ref[...] = jnp.zeros_like(ref)
        ref[:rows, :] = own_ref[:, at : at + ref.shape[1]]
        at += ref.shape[1]


def fetches(cuts, source_refs, out_refs, sems):
    return [
        pltpu.make_async_copy(source_refs[source].at[pl.ds(*rows), pl.ds(*columns)], out_refs[i], sems.at[i])
        for i, (source, rows, columns) in enumerate(cuts)
    ]


def load_kernel(*refs, sources, cuts, experts):
    out_refs = refs[sources + 1 : -1]
    copies = fetches(cuts, refs[:sources], out_refs, refs[-1])
    for copy in copies:
        copy.start()
    if experts:
        spread_ref = out_refs[-1]
        held = experts // lax.axis_size("expert")
        lane = lax.broadcasted_iota(jnp.int32, spread_ref.shape, 0)
        unit = lax.broadcasted_iota(jnp.int32, spread_ref.shape, 1)
        owner = lax.axis_index("expert") * held + unit // (spread_ref.shape[1] // held)
        hit = (lane == owner) | (lane == owner + experts) | (lane == owner + 2 * experts)
        spread_ref[...] = jnp.where(hit, 1.0, 0.0).astype(BF16)
    for copy in copies:
        copy.wait()


def loaded(cuts):
    return [pltpu.VMEM((rows[1], columns[1]), BF16) for _, rows, columns in cuts]


def load(arrays, cuts, after, experts=0, width=0):
    hidden = arrays[0].shape[0]
    outs = loaded(cuts) + [pltpu.VMEM((width, hidden), BF16)] * bool(experts)
    return pl.pallas_call(
        lambda *refs: load_kernel(*refs, sources=len(arrays), cuts=cuts, experts=experts),
        out_shape=outs,
        in_specs=[IN_HBM] * len(arrays) + [ANYWHERE],
        out_specs=[IN_VMEM] * len(outs),
        scratch_shapes=[pltpu.SemaphoreType.DMA((len(cuts),))],
        compiler_params=params(1),
        cost_estimate=NO_COST,
    )(*[far(a) for a in arrays], after)


def dot_rows(rows, matrix):
    return lax.dot_general(rows, matrix, (((1,), (1,)), ((), ())), preferred_element_type=F32)


def gate_up(rows, gate_ref, up_ref, at, block):
    here = slice(at, at + block)
    both = dot_rows(rows, jnp.concatenate([gate_ref[here], up_ref[here]], axis=0))
    return both[:, :block], both[:, block:]


def first_kernel(*refs, pieces, block):
    piece_refs = refs[:pieces]
    gate_ref, up_ref, rows_ref, gate_out, up_out = refs[pieces:]
    count = piece_refs[0].shape[0]
    for i, ref in enumerate(piece_refs):
        rows_ref[i * count : (i + 1) * count, :] = ref[...]
    for j in range(0, gate_out.shape[1], block):
        gate_out[:, j : j + block], up_out[:, j : j + block] = gate_up(rows_ref[...], gate_ref, up_ref, j, block)


def middle_kernel(rows_ref, gate_ref, up_ref, gate_out, up_out, *, block, start):
    for j in range(0, gate_out.shape[1], block):
        gate_out[:, j : j + block], up_out[:, j : j + block] = gate_up(
            rows_ref[...], gate_ref, up_ref, start + j, block
        )


def second_kernel(*refs, pieces, block, part, cuts):
    piece_refs = refs[:pieces]
    gate_ref, up_ref, *sums = refs[pieces : pieces + 6]
    spread_ref, down_hbm, act_ref, *down_refs, rows_ref, sems = refs[pieces + 6 :]
    copies = fetches(cuts, (down_hbm,), down_refs, sems)
    for copy in copies:
        copy.start()
    count = piece_refs[0].shape[0]
    for i, ref in enumerate(piece_refs):
        rows_ref[i * count : (i + 1) * count, :] = ref[...]
    cut = sums[0].shape[1]
    for j in range(0, gate_ref.shape[0], block):
        here = slice(j, j + block)
        gate, up = gate_up(rows_ref[:, :part], gate_ref, up_ref, j, block)
        weight = jnp.dot(rows_ref[:, part:], spread_ref[:, here], preferred_element_type=F32)
        gate_in, up_in = sums[:2] if j < cut else sums[2:]
        at = j if j < cut else j - cut
        gate, up = gate + gate_in[:, at : at + block], up + up_in[:, at : at + block]
        act_ref[:, here] = (gate / (1.0 + jnp.exp(-gate)) * up * weight).astype(BF16)
    for copy in copies:
        copy.wait()


def down_kernel(act_ref, down_ref, keep_ref, send_ref, *, chunk):
    half = keep_ref.shape[0]
    for j in range(keep_ref.shape[1] // chunk):
        here = slice(j * chunk, (j + 1) * chunk)
        out = jnp.dot(act_ref[...], down_ref[:, here], preferred_element_type=F32)
        keep_ref[:, here] = out[:half]
        send_ref[:, here] = out[half:].astype(BF16)


def params(mib):
    return pltpu.CompilerParams(vmem_limit_bytes=mib * MIB)


NO_COST = pl.CostEstimate(flops=0, bytes_accessed=0, transcendentals=0)


def local(stream_in, norm_gain, expert_ids, route_weights, w_gate, w_up, w_down):
    row_count, features = stream_in.shape
    held, slice_size, _ = w_gate.shape
    attn_size = lax.axis_size("attn")
    expert_size = lax.axis_size("expert")
    experts = held * expert_size
    width = -(-3 * experts // LANES) * LANES
    hidden = held * slice_size
    rest = features - AG_CUT
    tokens = row_count * attn_size * expert_size
    half = tokens // 2
    steps = (expert_size // 2).bit_length() - 1
    cut = ROWS_FIRST * hidden // 1536
    every = (0, hidden)
    beside = lambda i: i ^ 1

    w_gate = w_gate.reshape(hidden, features)
    w_up = w_up.reshape(hidden, features)
    w_down = w_down.reshape(hidden, features)

    own, column = pl.pallas_call(
        lambda *refs: pack_kernel(*refs, experts=experts),
        out_shape=[
            pltpu.VMEM((row_count, features + width), BF16),
            pltpu.VMEM((row_count * attn_size, features + width), BF16),
        ],
    )(stream_in, norm_gain.reshape(features // LANES, LANES), expert_ids, route_weights)

    received = {d: swap(own, "attn", hop(d, attn_size)) for d in order_of(AG_ORDER, attn_size)}
    (gate_1,) = load([w_gate], [(0, every, (0, AG_CUT))], own)
    *values, gate_1 = lax.optimization_barrier((*received.values(), gate_1))
    for d, value in zip(received, values):
        column = column.at[d * row_count : (d + 1) * row_count].set(value)

    gate_2, up_1 = load([w_gate, w_up], [(0, every, (AG_CUT, rest)), (1, every, (0, AG_CUT))], column)
    columns = [column[:, :AG_CUT], column[:, AG_CUT:]] if P1_SPLIT else [column]
    for step in range(steps - 1):
        others = [swap(value, "expert", partner(step, steps)) for value in columns]
        if step == 0:
            others[0], gate_2, up_1 = lax.optimization_barrier((others[0], gate_2, up_1))
        columns = [jnp.concatenate(pair, axis=0) for pair in zip(columns, others)]
    if not P1_SPLIT:
        columns = [columns[0][:, :AG_CUT], columns[0][:, AG_CUT:]]
    up_2, spread = load([w_up], [(0, every, (AG_CUT, rest))], columns[0], experts, width)
    others = [swap(value, "expert", partner(steps - 1, steps)) for value in columns]
    others[0], up_2, spread = lax.optimization_barrier((others[0], up_2, spread))

    def both_of_pair(pieces):
        return pieces + [swap(piece, "expert", beside) for piece in pieces]

    pieces = both_of_pair([columns[0], others[0]])
    count = len(pieces)
    rows, gate_a, up_a = pl.pallas_call(
        lambda *refs: first_kernel(*refs, pieces=count, block=LANES),
        out_shape=[pltpu.VMEM((tokens, AG_CUT), BF16)] + [pltpu.VMEM((tokens, cut), F32)] * 2,
        in_specs=[IN_VMEM] * (count + 2),
        out_specs=[IN_VMEM] * 3,
        compiler_params=params(6),
        cost_estimate=NO_COST,
    )(*pieces, near(gate_1), near(up_1))
    others[1], rows = lax.optimization_barrier((others[1], rows))
    gate_b, up_b = pl.pallas_call(
        lambda *refs: middle_kernel(*refs, block=LANES, start=cut),
        out_shape=[pltpu.VMEM((tokens, hidden - cut), F32)] * 2,
        in_specs=[IN_VMEM] * 3,
        out_specs=[IN_VMEM] * 2,
        compiler_params=params(6),
        cost_estimate=NO_COST,
    )(near(rows), near(gate_1), near(up_1))
    pieces = both_of_pair([columns[1], others[1]])
    starts = [sum(RS_CUTS[:i]) for i in range(len(RS_CUTS))]
    cuts = [(0, every, (at, size)) for at, size in zip(starts, RS_CUTS)]
    act, *downs = pl.pallas_call(
        lambda *refs: second_kernel(*refs, pieces=count, block=LANES, part=rest, cuts=cuts),
        out_shape=[pltpu.VMEM((tokens, hidden), BF16)] + loaded(cuts),
        in_specs=[IN_VMEM] * (count + 7) + [IN_HBM],
        out_specs=[IN_VMEM] * (1 + len(cuts)),
        scratch_shapes=[pltpu.VMEM((tokens, rest + width), BF16), pltpu.SemaphoreType.DMA((len(cuts),))],
        compiler_params=params(6),
        cost_estimate=NO_COST,
    )(
        *pieces,
        *[near(value) for value in (gate_2, up_2, gate_a, up_a, gate_b, up_b, spread)],
        far(w_down),
    )

    outs = []
    for size, down in zip(RS_CUTS, downs):
        keep, send = pl.pallas_call(
            lambda *refs: down_kernel(*refs, chunk=512),
            out_shape=[pltpu.VMEM((half, size), F32), pltpu.VMEM((half, size), BF16)],
            in_specs=[IN_VMEM] * 2,
            out_specs=[IN_VMEM] * 2,
            compiler_params=params(12),
            cost_estimate=NO_COST,
        )(near(act), near(down))
        total = keep + swap(send, "expert", beside).astype(F32)
        for step in reversed(range(steps)):
            total = fold(total, step, steps)
        outs.append(total)
    total = jnp.concatenate(outs, axis=1).reshape(attn_size, row_count, features)
    back = [swap(total[d].astype(BF16), "attn", hop(-d, attn_size)) for d in order_of(RS_ORDER, attn_size)]
    return sum([value.astype(F32) for value in back], total[0])


def solution(mesh):
    return jax.shard_map(
        local,
        mesh=mesh,
        in_specs=(
            P(("attn", "expert"), None),
            P(),
            P(("attn", "expert"), None),
            P(("attn", "expert"), None),
            P("expert", "attn", None),
            P("expert", "attn", None),
            P("expert", "attn", None),
        ),
        out_specs=P(("attn", "expert"), None),
        check_vma=False,
    )
```

```python
import jax
import jax.numpy as jnp
from jax import lax
from jax.experimental import pallas as pl
from jax.experimental.pallas import tpu as pltpu
from jax.sharding import PartitionSpec as P

LANES = 128
F32 = jnp.float32
BF16 = jnp.bfloat16
MIB = 1 << 20
AG_CUT = 1792
RS_CUTS = (2048, 2048)
EARLY = 256
ROWS_FIRST = 768
AG_ORDER = (1, 2, 3)
RS_ORDER = (2, 3, 1)
IN_VMEM = pl.BlockSpec(memory_space=pltpu.VMEM)
IN_HBM = pl.BlockSpec(memory_space=pltpu.HBM)
ANYWHERE = pl.BlockSpec(memory_space=pl.ANY)


def near(value):
    return pltpu.with_memory_space_constraint(value, pltpu.VMEM)


def far(value):
    return pltpu.with_memory_space_constraint(value, pltpu.HBM)


def swap(value, axis, to):
    return lax.ppermute(value, axis, [(i, to(i)) for i in range(lax.axis_size(axis))])


def hop(distance, size):
    return lambda i: (i + distance) % size


def order_of(order, size):
    return order if len(order) == size - 1 else range(size - 1, 0, -1)


def partner(step, steps):
    return lambda i: i ^ (2 << (step if i % 2 == 0 else steps - 1 - step))


def fold(total, step, steps):
    count = total.shape[0] // 2
    back = swap(total[count:].astype(BF16), "expert", partner(step, steps))
    return total[:count] + back.astype(F32)


def pack_kernel(stream_ref, gain_ref, ids_ref, weights_ref, own_ref, column_ref, *, experts):
    stream = stream_ref[...].astype(F32)
    inverse = lax.rsqrt(jnp.mean(stream * stream, axis=-1, keepdims=True) + 1e-06)
    rows, features = stream.shape
    blank = column_ref.shape[0] - rows

    def put(value, here):
        own_ref[:, here] = value.astype(BF16)
        empty = jnp.zeros((blank, value.shape[1]), F32)
        column_ref[:, here] = jnp.concatenate([value, empty], axis=0).astype(BF16)

    for i in range(features // LANES):
        here = slice(i * LANES, (i + 1) * LANES)
        put(stream[:, here] * inverse * gain_ref[i : i + 1, :].astype(F32), here)
    width = own_ref.shape[1] - features
    column = lax.broadcasted_iota(jnp.int32, (rows, width), 1)
    dense = jnp.zeros((rows, width), F32)
    for k in range(ids_ref.shape[1]):
        expert = ids_ref[:, k : k + 1]
        weight = weights_ref[:, k : k + 1]
        high = weight.astype(BF16).astype(F32)
        middle = (weight - high).astype(BF16).astype(F32)
        low = weight - high - middle
        dense = dense + jnp.where(column == expert, high, 0.0)
        dense = dense + jnp.where(column == expert + experts, middle, 0.0)
        dense = dense + jnp.where(column == expert + 2 * experts, low, 0.0)
    put(dense, slice(features, features + width))


def fetches(cuts, source_refs, out_refs, sems):
    return [
        pltpu.make_async_copy(source_refs[source].at[pl.ds(*rows), pl.ds(*columns)], out_refs[i], sems.at[i])
        for i, (source, rows, columns) in enumerate(cuts)
    ]


def load_kernel(*refs, sources, cuts, experts):
    out_refs = refs[sources + 1 : -1]
    copies = fetches(cuts, refs[:sources], out_refs, refs[-1])
    for copy in copies:
        copy.start()
    if experts:
        spread_ref = out_refs[-1]
        held = experts // lax.axis_size("expert")
        lane = lax.broadcasted_iota(jnp.int32, spread_ref.shape, 0)
        unit = lax.broadcasted_iota(jnp.int32, spread_ref.shape, 1)
        owner = lax.axis_index("expert") * held + unit // (spread_ref.shape[1] // held)
        hit = (lane == owner) | (lane == owner + experts) | (lane == owner + 2 * experts)
        spread_ref[...] = jnp.where(hit, 1.0, 0.0).astype(BF16)
    for copy in copies:
        copy.wait()


def loaded(cuts):
    return [pltpu.VMEM((rows[1], columns[1]), BF16) for _, rows, columns in cuts]


def load(arrays, cuts, after, experts=0, width=0):
    hidden = arrays[0].shape[0]
    outs = loaded(cuts) + [pltpu.VMEM((width, hidden), BF16)] * bool(experts)
    return pl.pallas_call(
        lambda *refs: load_kernel(*refs, sources=len(arrays), cuts=cuts, experts=experts),
        out_shape=outs,
        in_specs=[IN_HBM] * len(arrays) + [ANYWHERE],
        out_specs=[IN_VMEM] * len(outs),
        scratch_shapes=[pltpu.SemaphoreType.DMA((len(cuts),))],
        compiler_params=params(1),
        cost_estimate=NO_COST,
    )(*[far(a) for a in arrays], after)


def dot_rows(rows, matrix):
    return lax.dot_general(rows, matrix, (((1,), (1,)), ((), ())), preferred_element_type=F32)


def gate_up(rows, gate_ref, up_ref, at, block):
    here = slice(at, at + block)
    both = dot_rows(rows, jnp.concatenate([gate_ref[here], up_ref[here]], axis=0))
    return both[:, :block], both[:, block:]


def first_kernel(*refs, pieces, block):
    piece_refs = refs[:pieces]
    gate_ref, up_ref, rows_ref, gate_out, up_out = refs[pieces:]
    count = piece_refs[0].shape[0]
    for i, ref in enumerate(piece_refs):
        rows_ref[i * count : (i + 1) * count, :] = ref[...]
    for j in range(0, gate_out.shape[1], block):
        gate_out[:, j : j + block], up_out[:, j : j + block] = gate_up(rows_ref[...], gate_ref, up_ref, j, block)


def middle_kernel(rows_ref, gate_ref, up_ref, gate_out, up_out, *, block, start):
    for j in range(0, gate_out.shape[1], block):
        gate_out[:, j : j + block], up_out[:, j : j + block] = gate_up(
            rows_ref[...], gate_ref, up_ref, start + j, block
        )


def second_kernel(*refs, pieces, block, part, cuts):
    piece_refs = refs[:pieces]
    gate_ref, up_ref, *sums = refs[pieces : pieces + 6]
    spread_ref, down_hbm, act_ref, *down_refs, rows_ref, sems = refs[pieces + 6 :]
    copies = fetches(cuts, (down_hbm,), down_refs, sems)
    for copy in copies:
        copy.start()
    count = piece_refs[0].shape[0]
    for i, ref in enumerate(piece_refs):
        rows_ref[i * count : (i + 1) * count, :] = ref[...]
    cut = sums[0].shape[1]
    for j in range(0, gate_ref.shape[0], block):
        here = slice(j, j + block)
        gate, up = gate_up(rows_ref[:, :part], gate_ref, up_ref, j, block)
        weight = jnp.dot(rows_ref[:, part:], spread_ref[:, here], preferred_element_type=F32)
        gate_in, up_in = sums[:2] if j < cut else sums[2:]
        at = j if j < cut else j - cut
        gate, up = gate + gate_in[:, at : at + block], up + up_in[:, at : at + block]
        act_ref[:, here] = (gate / (1.0 + jnp.exp(-gate)) * up * weight).astype(BF16)
    for copy in copies:
        copy.wait()


def down_kernel(act_ref, *refs, chunk, start):
    *down_refs, keep_ref, send_ref = refs
    half = keep_ref.shape[0]
    depths = [ref.shape[0] for ref in down_refs]
    starts = [sum(depths[:i]) for i in range(len(depths))]
    for j in range(0, keep_ref.shape[1], chunk):
        here, there = slice(j, j + chunk), slice(start + j, start + j + chunk)
        out = sum(
            jnp.dot(act_ref[:, at : at + depth], ref[:, there], preferred_element_type=F32)
            for at, depth, ref in zip(starts, depths, down_refs)
        )
        keep_ref[:, here] = out[:half]
        send_ref[:, here] = out[half:].astype(BF16)


def params(mib):
    return pltpu.CompilerParams(vmem_limit_bytes=mib * MIB)


NO_COST = pl.CostEstimate(flops=0, bytes_accessed=0, transcendentals=0)


def local(stream_in, norm_gain, expert_ids, route_weights, w_gate, w_up, w_down):
    row_count, features = stream_in.shape
    held, slice_size, _ = w_gate.shape
    attn_size = lax.axis_size("attn")
    expert_size = lax.axis_size("expert")
    experts = held * expert_size
    width = -(-3 * experts // LANES) * LANES
    hidden = held * slice_size
    rest = features - AG_CUT
    tokens = row_count * attn_size * expert_size
    half = tokens // 2
    steps = (expert_size // 2).bit_length() - 1
    cut = ROWS_FIRST * hidden // 1536
    every = (0, hidden)
    beside = lambda i: i ^ 1

    w_gate = w_gate.reshape(hidden, features)
    w_up = w_up.reshape(hidden, features)
    w_down = w_down.reshape(hidden, features)

    own, column = pl.pallas_call(
        lambda *refs: pack_kernel(*refs, experts=experts),
        out_shape=[
            pltpu.VMEM((row_count, features + width), BF16),
            pltpu.VMEM((row_count * attn_size, features + width), BF16),
        ],
    )(stream_in, norm_gain.reshape(features // LANES, LANES), expert_ids, route_weights)

    received = {d: swap(own, "attn", hop(d, attn_size)) for d in order_of(AG_ORDER, attn_size)}
    early = EARLY * hidden // 1536
    cuts = [(0, every, (0, AG_CUT)), (1, (0, early), (0, features))]
    gate_1, *downs_1 = load([w_gate, w_down], cuts, own)
    *values, gate_1 = lax.optimization_barrier((*received.values(), gate_1))
    for d, value in zip(received, values):
        column = column.at[d * row_count : (d + 1) * row_count].set(value)

    gate_2, up_1 = load([w_gate, w_up], [(0, every, (AG_CUT, rest)), (1, every, (0, AG_CUT))], column)
    columns = [column]
    for step in range(steps - 1):
        others = [swap(value, "expert", partner(step, steps)) for value in columns]
        if step == 0:
            others[0], gate_2, up_1 = lax.optimization_barrier((others[0], gate_2, up_1))
        columns = [jnp.concatenate(pair, axis=0) for pair in zip(columns, others)]
    columns = [columns[0][:, :AG_CUT], columns[0][:, AG_CUT:]]
    up_2, spread = load([w_up], [(0, every, (AG_CUT, rest))], columns[0], experts, width)
    others = [swap(value, "expert", partner(steps - 1, steps)) for value in columns]
    others[0], up_2, spread = lax.optimization_barrier((others[0], up_2, spread))

    def both_of_pair(pieces):
        return pieces + [swap(piece, "expert", beside) for piece in pieces]

    pieces = both_of_pair([columns[0], others[0]])
    count = len(pieces)
    rows, gate_a, up_a = pl.pallas_call(
        lambda *refs: first_kernel(*refs, pieces=count, block=LANES),
        out_shape=[pltpu.VMEM((tokens, AG_CUT), BF16)] + [pltpu.VMEM((tokens, cut), F32)] * 2,
        in_specs=[IN_VMEM] * (count + 2),
        out_specs=[IN_VMEM] * 3,
        compiler_params=params(6),
        cost_estimate=NO_COST,
    )(*pieces, near(gate_1), near(up_1))
    others[1], rows = lax.optimization_barrier((others[1], rows))
    gate_b, up_b = pl.pallas_call(
        lambda *refs: middle_kernel(*refs, block=LANES, start=cut),
        out_shape=[pltpu.VMEM((tokens, hidden - cut), F32)] * 2,
        in_specs=[IN_VMEM] * 3,
        out_specs=[IN_VMEM] * 2,
        compiler_params=params(6),
        cost_estimate=NO_COST,
    )(near(rows), near(gate_1), near(up_1))
    pieces = both_of_pair([columns[1], others[1]])
    starts = [sum(RS_CUTS[:i]) for i in range(len(RS_CUTS))]
    cuts = [(0, (early, hidden - early), (0, features))]
    act, *downs_3 = pl.pallas_call(
        lambda *refs: second_kernel(*refs, pieces=count, block=LANES, part=rest, cuts=cuts),
        out_shape=[pltpu.VMEM((tokens, hidden), BF16)] + loaded(cuts),
        in_specs=[IN_VMEM] * (count + 7) + [IN_HBM],
        out_specs=[IN_VMEM] * (1 + len(cuts)),
        scratch_shapes=[pltpu.VMEM((tokens, rest + width), BF16), pltpu.SemaphoreType.DMA((len(cuts),))],
        compiler_params=params(6),
        cost_estimate=NO_COST,
    )(
        *pieces,
        *[near(value) for value in (gate_2, up_2, gate_a, up_a, gate_b, up_b, spread)],
        far(w_down),
    )

    downs = [*downs_1, *downs_3]
    outs = []
    for start, size in zip(starts, RS_CUTS):
        keep, send = pl.pallas_call(
            lambda *refs, start=start: down_kernel(*refs, chunk=512, start=start),
            out_shape=[pltpu.VMEM((half, size), F32), pltpu.VMEM((half, size), BF16)],
            in_specs=[IN_VMEM] * (1 + len(downs)),
            out_specs=[IN_VMEM] * 2,
            compiler_params=params(12),
            cost_estimate=NO_COST,
        )(near(act), *[near(down) for down in downs])
        total = keep + swap(send, "expert", beside).astype(F32)
        for step in reversed(range(steps)):
            total = fold(total, step, steps)
        outs.append(total)
    total = jnp.concatenate(outs, axis=1).reshape(attn_size, row_count, features)
    back = [swap(total[d].astype(BF16), "attn", hop(-d, attn_size)) for d in order_of(RS_ORDER, attn_size)]
    return sum([value.astype(F32) for value in back], total[0])


def solution(mesh):
    return jax.shard_map(
        local,
        mesh=mesh,
        in_specs=(
            P(("attn", "expert"), None),
            P(),
            P(("attn", "expert"), None),
            P(("attn", "expert"), None),
            P("expert", "attn", None),
            P("expert", "attn", None),
            P("expert", "attn", None),
        ),
        out_specs=P(("attn", "expert"), None),
        check_vma=False,
    )
```

```python
import jax
import jax.numpy as jnp
from jax import lax
from jax.experimental import pallas as pl
from jax.experimental.pallas import tpu as pltpu
from jax.sharding import PartitionSpec as P

LANES = 128
F32 = jnp.float32
BF16 = jnp.bfloat16
MIB = 1 << 20
AG_CUT = 1792
RS_CUTS = (2048, 2048)
EARLY = 256
ROWS_FIRST = 768
AG_ORDER = (1, 2, 3)
RS_ORDER = (2, 3, 1)
IN_VMEM = pl.BlockSpec(memory_space=pltpu.VMEM)
IN_HBM = pl.BlockSpec(memory_space=pltpu.HBM)
ANYWHERE = pl.BlockSpec(memory_space=pl.ANY)


def near(value):
    return pltpu.with_memory_space_constraint(value, pltpu.VMEM)


def far(value):
    return pltpu.with_memory_space_constraint(value, pltpu.HBM)


def swap(value, axis, to):
    return lax.ppermute(value, axis, [(i, to(i)) for i in range(lax.axis_size(axis))])


def hop(distance, size):
    return lambda i: (i + distance) % size


def order_of(order, size):
    return order if len(order) == size - 1 else range(size - 1, 0, -1)


def partner(step, steps):
    return lambda i: i ^ (2 << (step if i % 2 == 0 else steps - 1 - step))


def fold(total, step, steps):
    count = total.shape[0] // 2
    back = swap(total[count:].astype(BF16), "expert", partner(step, steps))
    return total[:count] + back.astype(F32)


def pack_kernel(stream_ref, gain_ref, ids_ref, weights_ref, own_ref, column_ref, *, experts):
    stream = stream_ref[...].astype(F32)
    inverse = lax.rsqrt(jnp.mean(stream * stream, axis=-1, keepdims=True) + 1e-06)
    rows, features = stream.shape
    blank = column_ref.shape[0] - rows

    def put(value, here):
        own_ref[:, here] = value.astype(BF16)
        empty = jnp.zeros((blank, value.shape[1]), F32)
        column_ref[:, here] = jnp.concatenate([value, empty], axis=0).astype(BF16)

    for i in range(features // LANES):
        here = slice(i * LANES, (i + 1) * LANES)
        put(stream[:, here] * inverse * gain_ref[i : i + 1, :].astype(F32), here)
    width = own_ref.shape[1] - features
    column = lax.broadcasted_iota(jnp.int32, (rows, width), 1)
    dense = jnp.zeros((rows, width), F32)
    for k in range(ids_ref.shape[1]):
        expert = ids_ref[:, k : k + 1]
        weight = weights_ref[:, k : k + 1]
        high = weight.astype(BF16).astype(F32)
        middle = (weight - high).astype(BF16).astype(F32)
        low = weight - high - middle
        dense = dense + jnp.where(column == expert, high, 0.0)
        dense = dense + jnp.where(column == expert + experts, middle, 0.0)
        dense = dense + jnp.where(column == expert + 2 * experts, low, 0.0)
    put(dense, slice(features, features + width))


def fetches(cuts, source_refs, out_refs, sems):
    return [
        pltpu.make_async_copy(source_refs[source].at[pl.ds(*rows), pl.ds(*columns)], out_refs[i], sems.at[i])
        for i, (source, rows, columns) in enumerate(cuts)
    ]


def load_kernel(*refs, sources, cuts, experts):
    out_refs = refs[sources + 1 : -1]
    copies = fetches(cuts, refs[:sources], out_refs, refs[-1])
    for copy in copies:
        copy.start()
    if experts:
        spread_ref = out_refs[-1]
        held = experts // lax.axis_size("expert")
        lane = lax.broadcasted_iota(jnp.int32, spread_ref.shape, 0)
        unit = lax.broadcasted_iota(jnp.int32, spread_ref.shape, 1)
        owner = lax.axis_index("expert") * held + unit // (spread_ref.shape[1] // held)
        hit = (lane == owner) | (lane == owner + experts) | (lane == owner + 2 * experts)
        spread_ref[...] = jnp.where(hit, 1.0, 0.0).astype(BF16)
    for copy in copies:
        copy.wait()


def loaded(cuts):
    return [pltpu.VMEM((rows[1], columns[1]), BF16) for _, rows, columns in cuts]


def load(arrays, cuts, after, experts=0, width=0):
    hidden = arrays[0].shape[0]
    outs = loaded(cuts) + [pltpu.VMEM((width, hidden), BF16)] * bool(experts)
    return pl.pallas_call(
        lambda *refs: load_kernel(*refs, sources=len(arrays), cuts=cuts, experts=experts),
        out_shape=outs,
        in_specs=[IN_HBM] * len(arrays) + [ANYWHERE],
        out_specs=[IN_VMEM] * len(outs),
        scratch_shapes=[pltpu.SemaphoreType.DMA((len(cuts),))],
        compiler_params=params(1),
        cost_estimate=NO_COST,
    )(*[far(a) for a in arrays], after)


def dot_rows(rows, matrix):
    return lax.dot_general(rows, matrix, (((1,), (1,)), ((), ())), preferred_element_type=F32)


def gate_up(rows, gate_ref, up_ref, at, block):
    here = slice(at, at + block)
    both = dot_rows(rows, jnp.concatenate([gate_ref[here], up_ref[here]], axis=0))
    return both[:, :block], both[:, block:]


def first_kernel(*refs, pieces, block):
    piece_refs = refs[:pieces]
    gate_ref, up_ref, rows_ref, gate_out, up_out = refs[pieces:]
    count = piece_refs[0].shape[0]
    for i, ref in enumerate(piece_refs):
        rows_ref[i * count : (i + 1) * count, :] = ref[...]
    for j in range(0, gate_out.shape[1], block):
        gate_out[:, j : j + block], up_out[:, j : j + block] = gate_up(rows_ref[...], gate_ref, up_ref, j, block)


def middle_kernel(rows_ref, gate_ref, up_ref, gate_out, up_out, *, block, start):
    for j in range(0, gate_out.shape[1], block):
        gate_out[:, j : j + block], up_out[:, j : j + block] = gate_up(
            rows_ref[...], gate_ref, up_ref, start + j, block
        )


def second_kernel(*refs, pieces, block, part, cuts):
    piece_refs = refs[:pieces]
    gate_ref, up_ref, *sums = refs[pieces : pieces + 6]
    spread_ref, down_hbm, act_ref, *down_refs, rows_ref, sems = refs[pieces + 6 :]
    copies = fetches(cuts, (down_hbm,), down_refs, sems)
    for copy in copies:
        copy.start()
    count = piece_refs[0].shape[0]
    for i, ref in enumerate(piece_refs):
        rows_ref[i * count : (i + 1) * count, :] = ref[...]
    cut = sums[0].shape[1]
    for j in range(0, gate_ref.shape[0], block):
        here = slice(j, j + block)
        gate, up = gate_up(rows_ref[:, :part], gate_ref, up_ref, j, block)
        weight = jnp.dot(rows_ref[:, part:], spread_ref[:, here], preferred_element_type=F32)
        gate_in, up_in = sums[:2] if j < cut else sums[2:]
        at = j if j < cut else j - cut
        gate, up = gate + gate_in[:, at : at + block], up + up_in[:, at : at + block]
        act_ref[:, here] = (gate / (1.0 + jnp.exp(-gate)) * up * weight).astype(BF16)
    for copy in copies:
        copy.wait()


def down_kernel(act_ref, *refs, chunk, start):
    *down_refs, keep_ref, send_ref = refs
    half = keep_ref.shape[0]
    depths = [ref.shape[0] for ref in down_refs]
    starts = [sum(depths[:i]) for i in range(len(depths))]
    for j in range(0, keep_ref.shape[1], chunk):
        here, there = slice(j, j + chunk), slice(start + j, start + j + chunk)
        out = sum(
            jnp.dot(act_ref[:, at : at + depth], ref[:, there], preferred_element_type=F32)
            for at, depth, ref in zip(starts, depths, down_refs)
        )
        keep_ref[:, here] = out[:half]
        send_ref[:, here] = out[half:].astype(BF16)


def params(mib):
    return pltpu.CompilerParams(vmem_limit_bytes=mib * MIB)


NO_COST = pl.CostEstimate(flops=0, bytes_accessed=0, transcendentals=0)


def local(stream_in, norm_gain, expert_ids, route_weights, w_gate, w_up, w_down):
    row_count, features = stream_in.shape
    held, slice_size, _ = w_gate.shape
    attn_size = lax.axis_size("attn")
    expert_size = lax.axis_size("expert")
    experts = held * expert_size
    width = -(-3 * experts // LANES) * LANES
    hidden = held * slice_size
    rest = features - AG_CUT
    tokens = row_count * attn_size * expert_size
    half = tokens // 2
    steps = (expert_size // 2).bit_length() - 1
    cut = ROWS_FIRST * hidden // 1536
    every = (0, hidden)
    block = 2 * LANES if cut % (2 * LANES) == 0 else LANES
    beside = lambda i: i ^ 1

    w_gate = w_gate.reshape(hidden, features)
    w_up = w_up.reshape(hidden, features)
    w_down = w_down.reshape(hidden, features)

    own, column = pl.pallas_call(
        lambda *refs: pack_kernel(*refs, experts=experts),
        out_shape=[
            pltpu.VMEM((row_count, features + width), BF16),
            pltpu.VMEM((row_count * attn_size, features + width), BF16),
        ],
    )(stream_in, norm_gain.reshape(features // LANES, LANES), expert_ids, route_weights)

    received = {d: swap(own, "attn", hop(d, attn_size)) for d in order_of(AG_ORDER, attn_size)}
    early = EARLY * hidden // 1536
    cuts = [(0, every, (0, AG_CUT)), (1, (0, early), (0, features))]
    gate_1, *downs_1 = load([w_gate, w_down], cuts, own)
    *values, gate_1 = lax.optimization_barrier((*received.values(), gate_1))
    for d, value in zip(received, values):
        column = column.at[d * row_count : (d + 1) * row_count].set(value)

    gate_2, up_1 = load([w_gate, w_up], [(0, every, (AG_CUT, rest)), (1, every, (0, AG_CUT))], column)
    columns = [column]
    for step in range(steps - 1):
        others = [swap(value, "expert", partner(step, steps)) for value in columns]
        if step == 0:
            others[0], gate_2, up_1 = lax.optimization_barrier((others[0], gate_2, up_1))
        columns = [jnp.concatenate(pair, axis=0) for pair in zip(columns, others)]
    columns = [columns[0][:, :AG_CUT], columns[0][:, AG_CUT:]]
    up_2, spread = load([w_up], [(0, every, (AG_CUT, rest))], columns[0], experts, width)
    others = [swap(value, "expert", partner(steps - 1, steps)) for value in columns]
    others[0], up_2, spread = lax.optimization_barrier((others[0], up_2, spread))

    def both_of_pair(pieces):
        return pieces + [swap(piece, "expert", beside) for piece in pieces]

    pieces = both_of_pair([columns[0], others[0]])
    count = len(pieces)
    rows, gate_a, up_a = pl.pallas_call(
        lambda *refs: first_kernel(*refs, pieces=count, block=block),
        out_shape=[pltpu.VMEM((tokens, AG_CUT), BF16)] + [pltpu.VMEM((tokens, cut), F32)] * 2,
        in_specs=[IN_VMEM] * (count + 2),
        out_specs=[IN_VMEM] * 3,
        compiler_params=params(6),
        cost_estimate=NO_COST,
    )(*pieces, near(gate_1), near(up_1))
    others[1], rows = lax.optimization_barrier((others[1], rows))
    gate_b, up_b = pl.pallas_call(
        lambda *refs: middle_kernel(*refs, block=block, start=cut),
        out_shape=[pltpu.VMEM((tokens, hidden - cut), F32)] * 2,
        in_specs=[IN_VMEM] * 3,
        out_specs=[IN_VMEM] * 2,
        compiler_params=params(6),
        cost_estimate=NO_COST,
    )(near(rows), near(gate_1), near(up_1))
    pieces = both_of_pair([columns[1], others[1]])
    starts = [sum(RS_CUTS[:i]) for i in range(len(RS_CUTS))]
    cuts = [(0, (early, hidden - early), (0, features))]
    act, *downs_3 = pl.pallas_call(
        lambda *refs: second_kernel(*refs, pieces=count, block=block, part=rest, cuts=cuts),
        out_shape=[pltpu.VMEM((tokens, hidden), BF16)] + loaded(cuts),
        in_specs=[IN_VMEM] * (count + 7) + [IN_HBM],
        out_specs=[IN_VMEM] * (1 + len(cuts)),
        scratch_shapes=[pltpu.VMEM((tokens, rest + width), BF16), pltpu.SemaphoreType.DMA((len(cuts),))],
        compiler_params=params(6),
        cost_estimate=NO_COST,
    )(
        *pieces,
        *[near(value) for value in (gate_2, up_2, gate_a, up_a, gate_b, up_b, spread)],
        far(w_down),
    )

    downs = [*downs_1, *downs_3]
    outs = []
    for start, size in zip(starts, RS_CUTS):
        keep, send = pl.pallas_call(
            lambda *refs, start=start: down_kernel(*refs, chunk=512, start=start),
            out_shape=[pltpu.VMEM((half, size), F32), pltpu.VMEM((half, size), BF16)],
            in_specs=[IN_VMEM] * (1 + len(downs)),
            out_specs=[IN_VMEM] * 2,
            compiler_params=params(12),
            cost_estimate=NO_COST,
        )(near(act), *[near(down) for down in downs])
        total = keep + swap(send, "expert", beside).astype(F32)
        for step in reversed(range(steps)):
            total = fold(total, step, steps)
        outs.append(total)
    total = jnp.concatenate(outs, axis=1).reshape(attn_size, row_count, features)
    back = [swap(total[d].astype(BF16), "attn", hop(-d, attn_size)) for d in order_of(RS_ORDER, attn_size)]
    return sum([value.astype(F32) for value in back], total[0])


def solution(mesh):
    return jax.shard_map(
        local,
        mesh=mesh,
        in_specs=(
            P(("attn", "expert"), None),
            P(),
            P(("attn", "expert"), None),
            P(("attn", "expert"), None),
            P("expert", "attn", None),
            P("expert", "attn", None),
            P("expert", "attn", None),
        ),
        out_specs=P(("attn", "expert"), None),
        check_vma=False,
    )
```
